32 devices in a mesh: ctx: 16 (over z, y, core), head: 2 (over x).
Axes of the slice: x: 2, y: 2, z: 4, core: 2. Of those that a mesh axis runs over, the one named last changes fastest.
Arguments:
- queries: bfloat16 [24, 4096, 128], P('head', 'ctx'), may hold values from -40 to 40
- keys: bfloat16 [24, 4096, 128], P('head', 'ctx'), may hold values from -12 to 12
- values: bfloat16 [24, 4096, 128], P('head', 'ctx'), may hold values from -8 to 8
- block_lists: int32 [64, 16], P('ctx'), may hold values from 0 to 63, all different within a row
- coarse_gate: bfloat16 [24, 4096], P('head', 'ctx'), may hold values from 0.5 to 4
Outputs:
- attended: bfloat16 [24, 4096, 128], P('head', 'ctx')
The draws below stay inside these ranges and needn't reach their ends.
Inputs may be any that keep to these rules, and one draw needn't show every extreme that they name: `block_lists`: each row names 16 different key cubes, and every cube is named by some row.
All inputs are finite; a program needn't handle non-finite values.
Results may differ from the reference program's by a relative error of at most 0.0045.
The reference program's roundings to bfloat16 on the way count: a program that leaves them out, or rounds other values in their place, can miss the bound.
Values may be sent and summed in bfloat16 or wider, within the bound.
No kernel may reach another device: no remote copies, remote signals or barrier semaphores. Data moves between devices by JAX's collectives and lax.ppermute only.
A program may use at most 128 MiB of HBM per device.

```python
import math
import jax
import jax.numpy as jnp
from jax import lax

HEADS = 24
HD = 128
CUBE = 64
TOPK = 16
NCUBES = 64
TOKENS = 4096


def cube_layout(offset, noise):
    shaped = offset[:, :, None, :] + noise.reshape(HEADS, NCUBES, CUBE, HD)
    return shaped.reshape(HEADS, TOKENS, HD)


def draw_queries(key, part):
    key = jax.random.fold_in(key, 1)
    first, second = jax.random.split(key)
    offset = 0.7 * jax.random.normal(first, (HEADS, NCUBES, HD), jnp.float32)
    noise = 0.7 * jax.random.normal(second, (HEADS, TOKENS, HD), jnp.float32)
    result = cube_layout(offset, noise)
    return jnp.clip(result, -40.0, 40.0).astype(jnp.bfloat16)


def draw_keys(key, part):
    key = jax.random.fold_in(key, 2)
    first, second = jax.random.split(key)
    offset = 0.7 * jax.random.normal(first, (HEADS, NCUBES, HD), jnp.float32)
    noise = 0.7 * jax.random.normal(second, (HEADS, TOKENS, HD), jnp.float32)
    result = cube_layout(offset, noise)
    return jnp.clip(result, -12.0, 12.0).astype(jnp.bfloat16)


def draw_values(key, part):
    key = jax.random.fold_in(key, 3)
    first, second = jax.random.split(key)
    offset = 0.7 * jax.random.normal(first, (HEADS, NCUBES, HD), jnp.float32)
    noise = 0.7 * jax.random.normal(second, (HEADS, TOKENS, HD), jnp.float32)
    return jnp.clip(cube_layout(offset, noise), -8.0, 8.0).astype(jnp.bfloat16)


def level_of(rng, extent, cuts, least, largest):
    level, own = 1.0, jax.random.fold_in(rng, 6)
    for dim, shards_of in cuts:
        steps = jnp.exp(jax.random.uniform(jax.random.fold_in(own, dim), (shards_of,), jnp.float32, least / len(cuts), largest / len(cuts)))
        level = level * jnp.repeat(steps, extent[dim] // shards_of).reshape([-1 if axis == dim else 1 for axis in range(len(extent))])
    return level


def picks_of(rng, rows, number_of, top, lift):
    order = jax.random.permutation(jax.random.fold_in(rng, 1), number_of)
    boost = order
    for power in range(3):
        boost = boost * boost // number_of
    boost = boost * lift // number_of
    chance = jax.random.randint(jax.random.fold_in(rng, 2), (rows, number_of), 0, 4096) + boost
    fixed_rows = jax.random.permutation(jax.random.fold_in(rng, 3), rows)[jnp.arange(number_of) % rows]
    chance = jnp.where(jnp.arange(rows)[:, None] == fixed_rows[None, :], 1 << 14, chance)
    score = chance * number_of + jnp.arange(number_of)
    return lax.top_k(score.astype(jnp.int32), top)[1].astype(jnp.int32)


def setup_inputs(seed: int = 0) -> dict:
    seeds = jax.random.split(jax.random.key(seed), 6)
    return {
        "queries": draw_queries(jax.random.fold_in(seeds[5], 71), 0),
        "keys": draw_keys(jax.random.fold_in(seeds[5], 71), 0),
        "values": draw_values(jax.random.fold_in(seeds[5], 71), 0),
        "block_lists": picks_of(seeds[3], NCUBES, NCUBES, TOPK, 2048),
        "coarse_gate": jnp.clip(jnp.exp(math.log(4.0) - 2.0794415 * jax.random.uniform(seeds[4], (HEADS, TOKENS), jnp.float32) ** level_of(seeds[4], (HEADS, TOKENS), ((0, 2), (1, 16)), -0.2, 0.2)), 0.5, 4.0).astype(jnp.bfloat16),
    }


def pool_cubes(field):
    heads, tokens, width = field.shape
    pooled = lax.optimization_barrier(jnp.mean(field.astype(jnp.float32).reshape(heads, tokens // CUBE, CUBE, width), axis=2))
    return pooled.astype(jnp.bfloat16)

def reference(queries, keys, values, block_lists, coarse_gate):
    scale = 1.0 / math.sqrt(HD)
    pooled_q = pool_cubes(queries)
    pooled_k = pool_cubes(keys)
    pooled_v = pool_cubes(values)
    coarse_scores = jnp.einsum('hqd,hkd->hqk', pooled_q.astype(jnp.float32), pooled_k.astype(jnp.float32)) * scale
    coarse_top = lax.optimization_barrier(jnp.max(coarse_scores, axis=-1, keepdims=True))
    coarse_weights = jnp.exp(coarse_scores - coarse_top).astype(jnp.bfloat16)
    coarse_total = lax.optimization_barrier(jnp.sum(coarse_weights.astype(jnp.float32), axis=-1))
    coarse_cube = jnp.einsum('hqk,hkd->hqd', coarse_weights.astype(jnp.float32), pooled_v.astype(jnp.float32)) / coarse_total[..., None]
    key_tiles = keys.reshape(HEADS, NCUBES, CUBE, HD)
    value_tiles = values.reshape(HEADS, NCUBES, CUBE, HD)
    query_tiles = queries.reshape(HEADS, NCUBES, CUBE, HD)

    def one_cube(index):
        listed = block_lists[index].astype(jnp.int32)
        chosen_k = jnp.take(key_tiles, listed, axis=1).reshape(HEADS, TOPK * CUBE, HD)
        chosen_v = jnp.take(value_tiles, listed, axis=1).reshape(HEADS, TOPK * CUBE, HD)
        own = lax.dynamic_index_in_dim(query_tiles, index, 1, keepdims=False)
        scores = jnp.einsum('hqd,hkd->hqk', own.astype(jnp.float32), chosen_k.astype(jnp.float32)) * scale
        top = lax.optimization_barrier(jnp.max(scores, axis=-1, keepdims=True))
        weights = jnp.exp(scores - top).astype(jnp.bfloat16)
        total = lax.optimization_barrier(jnp.sum(weights.astype(jnp.float32), axis=-1))
        summed = jnp.einsum('hqk,hkd->hqd', weights.astype(jnp.float32), chosen_v.astype(jnp.float32))
        return summed / total[..., None]
    fine = lax.map(one_cube, jnp.arange(NCUBES, dtype=jnp.int32))
    fine_out = jnp.transpose(fine, (1, 0, 2, 3)).reshape(HEADS, TOKENS, HD)
    coarse_tokens = jnp.repeat(coarse_cube, CUBE, axis=1)
    return (fine_out + coarse_gate.astype(jnp.float32)[..., None] * coarse_tokens).astype(jnp.bfloat16)
```

```python
import functools
import math

import jax
import jax.numpy as jnp
from jax import lax
from jax.experimental import pallas as pl
from jax.experimental.pallas import tpu as pltpu
from jax.sharding import PartitionSpec as P

CUBE = 64
NEG = -1e30
LEVELS = 32766.0


def pool_cubes(field):
    heads, tokens, width = field.shape
    summed = jnp.sum(field.reshape(heads, tokens // CUBE, CUBE, width), axis=2, dtype=jnp.float32)
    return (summed / CUBE).astype(jnp.bfloat16)


def attend_kernel(blocks, factor, bias_ref, own_q_ref, far_q_ref, *refs):
    kv_refs = refs[:blocks]
    own_acc_ref, far_code_ref, own_stat_ref, far_stat_ref = refs[blocks : blocks + 4]
    score_ref = refs[blocks + 4]
    rows, width = own_q_ref.shape[1:]
    span = kv_refs[0].shape[2]
    cubes = rows // CUBE
    values = jnp.concatenate([ref[1, 0] for ref in kv_refs], axis=0)
    values = jnp.concatenate([values, jnp.ones_like(values)], axis=1)
    for half, q_ref in enumerate((own_q_ref, far_q_ref)):
        query = q_ref[0]
        top = jnp.full((rows, span), NEG, jnp.float32)
        for b in range(blocks):
            scores = lax.dot_general(
                query,
                kv_refs[b][0, 0],
                (((1,), (1,)), ((), ())),
                preferred_element_type=jnp.float32,
            )
            bias = bias_ref[half * cubes : (half + 1) * cubes, b * span : (b + 1) * span]
            scores = (scores.reshape(cubes, CUBE, span) + bias[:, None, :]).reshape(rows, span)
            top = jnp.maximum(top, scores)
            score_ref[:, b * span : (b + 1) * span] = scores
        top = jnp.max(top, axis=1, keepdims=True)
        weights = jnp.exp2((score_ref[...] - top) * factor).astype(jnp.bfloat16)
        both = jnp.dot(weights, values, preferred_element_type=jnp.float32)
        acc, total = both[:, :width], both[:, width:]
        lane = lax.broadcasted_iota(jnp.int32, (rows, width), 1)
        stats = jnp.where(lane == 0, top, total)
        if half == 0:
            own_acc_ref[0] = acc
            own_stat_ref[0] = jnp.transpose(stats)[:8]
        else:
            peak = jnp.max(jnp.abs(acc), axis=1, keepdims=True)
            step = jnp.maximum(peak, 1e-30) / LEVELS
            stats = jnp.where(lane == 2, step, stats)
            far_stat_ref[0] = jnp.transpose(stats)[:8]
            code = jnp.floor(acc / step + 0.5).astype(jnp.int32)
            far_code_ref[0] = code.astype(jnp.int16)


def attend(first, bias, queries, far_q, kvs):
    heads, rows, width = far_q.shape
    blocks = len(kvs)
    span = kvs[0].shape[2]
    factor = math.log2(math.e) / math.sqrt(width)
    head_block = pl.BlockSpec((1, rows, width), lambda h: (h, 0, 0))
    stat_block = pl.BlockSpec((1, 8, rows), lambda h: (h, 0, 0))
    work = heads * 2 * rows * blocks * span
    return pl.pallas_call(
        functools.partial(attend_kernel, blocks, factor),
        grid=(heads,),
        in_specs=[
            pl.BlockSpec(bias.shape, lambda h: (0, 0)),
            pl.BlockSpec((1, rows, width), lambda h: (first + h, 0, 0)),
            head_block,
        ]
        + [pl.BlockSpec((2, 1, span, width), lambda h: (0, h, 0, 0))] * blocks,
        out_specs=[head_block, head_block, stat_block, stat_block],
        out_shape=[
            jax.ShapeDtypeStruct((heads, rows, width), jnp.float32),
            jax.ShapeDtypeStruct((heads, rows, width), jnp.int16),
            jax.ShapeDtypeStruct((heads, 8, rows), jnp.float32),
            jax.ShapeDtypeStruct((heads, 8, rows), jnp.float32),
        ],
        scratch_shapes=[pltpu.VMEM((rows, blocks * span), jnp.float32)],
        compiler_params=pltpu.CompilerParams(vmem_limit_bytes=48 * 1024 * 1024),
        cost_estimate=pl.CostEstimate(
            flops=work * width * 4, bytes_accessed=heads * rows * width * 2 * (2 * blocks + 5), transcendentals=work
        ),
    )(bias, queries, far_q, *kvs)


def body(ring, queries, keys, values, block_lists, coarse_gate):
    heads, rows, width = queries.shape
    cubes = rows // CUBE
    scale = 1.0 / math.sqrt(width)
    factor = math.log2(math.e) * scale
    half = ring // 2
    me = lax.axis_index("ctx")
    lower = [1 << bit for bit in reversed(range(half.bit_length() - 1))]

    def swap(array, bit):
        return lax.ppermute(array, "ctx", [(i, i ^ bit) for i in range(ring)])

    pooled_q = pool_cubes(queries)
    pooled = jnp.concatenate([pool_cubes(keys), pool_cubes(values)], axis=2)[:, None]
    for bit in [1 << b for b in range(ring.bit_length() - 1)]:
        pooled = jnp.concatenate([pooled, swap(pooled, bit)], axis=1)
    pooled = pooled.reshape(heads, ring * cubes, 2 * width)
    coarse_scores = (
        jnp.einsum(
            "hqd,hkd->hqk", pooled_q, pooled[..., :width], preferred_element_type=jnp.float32
        )
        * scale
    )
    coarse_top = jnp.max(coarse_scores, axis=-1, keepdims=True)
    coarse_weights = jnp.exp(coarse_scores - coarse_top).astype(jnp.bfloat16)
    coarse_total = jnp.sum(coarse_weights.astype(jnp.float32), axis=-1)
    coarse_cube = (
        jnp.einsum(
            "hqk,hkd->hqd", coarse_weights, pooled[..., width:], preferred_element_type=jnp.float32
        )
        / coarse_total[..., None]
    )

    lists = jnp.concatenate([block_lists, swap(block_lists, half)], axis=0)
    masks = [0]
    for bit in lower:
        masks = masks + [m ^ bit for m in masks]
    lanes = jnp.concatenate(
        [(me ^ m) * cubes + jnp.arange(rows, dtype=jnp.int32) // CUBE for m in masks]
    )
    hit = jnp.any(lists[:, :, None] == lanes[None, None, :], axis=1)
    bias = jnp.where(hit, 0.0, NEG).astype(jnp.float32)

    parts = 4 if heads % 4 == 0 else 1
    each = heads // parts
    results = []
    for part in range(parts):
        first = part * each
        chosen = slice(first, first + each)
        far_q = swap(queries[chosen], half)
        kvs = [jnp.stack([keys[chosen], values[chosen]])]
        for bit in lower:
            kvs = kvs + [swap(kv, bit) for kv in kvs]
        own_acc, far_code, own_stat, far_stat = attend(first, bias, queries, far_q, kvs)
        code = swap(far_code, half)
        stat = swap(far_stat, half)
        best = jnp.maximum(own_stat[:, 0], stat[:, 0])
        own_share = jnp.exp2((own_stat[:, 0] - best) * factor)
        far_share = jnp.exp2((stat[:, 0] - best) * factor)
        total = own_share * own_stat[:, 1] + far_share * stat[:, 1]
        own_share = own_share / total
        far_share = far_share * stat[:, 2] / total
        fine = own_acc * own_share[..., None] + code.astype(jnp.float32) * far_share[..., None]
        coarse = jnp.repeat(coarse_cube[chosen], CUBE, axis=1)
        gate = coarse_gate[chosen].astype(jnp.float32)[..., None]
        results.append((fine + gate * coarse).astype(jnp.bfloat16))
    return jnp.concatenate(results, axis=0)


def solution(mesh):
    in_specs = (
        P("head", "ctx", None),
        P("head", "ctx", None),
        P("head", "ctx", None),
        P("ctx", None),
        P("head", "ctx"),
    )
    out_specs = P("head", "ctx", None)
    return jax.shard_map(
        functools.partial(body, mesh.shape["ctx"]),
        mesh=mesh,
        in_specs=in_specs,
        out_specs=out_specs,
        check_vma=False,
    )
```

```python
import functools
import math

import jax
import jax.numpy as jnp
from jax import lax
from jax.experimental import pallas as pl
from jax.experimental.pallas import tpu as pltpu
from jax.sharding import PartitionSpec as P

CUBE = 64
NEG = -1e30
LEVELS = 32766.0
FRACTION = 32767.0


def pool_cubes(field):
    heads, tokens, width = field.shape
    summed = jnp.sum(field.reshape(heads, tokens // CUBE, CUBE, width), axis=2, dtype=jnp.float32)
    return (summed / CUBE).astype(jnp.bfloat16)


def pack_kernel(spans, core_ref, keys_ref, values_ref, got_ref, *pack_refs):
    tokens = keys_ref.shape[1]
    share = got_ref.shape[1]
    for (first, size), pack_ref in zip(spans, pack_refs):
        heads = pl.ds(core_ref[0] * share + first, size)
        pack_ref[0, :, :tokens] = keys_ref[heads]
        pack_ref[1, :, :tokens] = values_ref[heads]
        pack_ref[:, :, tokens:] = got_ref[:, first : first + size]


def pack_groups(spans, core, keys, values, got):
    tokens, width = keys.shape[1:]

    def whole(shape):
        return pl.BlockSpec(tuple(shape), lambda h, core: (0,) * len(shape))

    outs = [jax.ShapeDtypeStruct((2, size, 2 * tokens, width), keys.dtype) for _, size in spans]
    return pl.pallas_call(
        functools.partial(pack_kernel, spans),
        grid_spec=pltpu.PrefetchScalarGridSpec(
            num_scalar_prefetch=1,
            grid=(1,),
            in_specs=[whole(a.shape) for a in (keys, values, got)],
            out_specs=[whole(out.shape) for out in outs],
        ),
        out_shape=outs,
        compiler_params=pltpu.CompilerParams(vmem_limit_bytes=24 * 1024 * 1024),
    )(core[None], keys, values, got)


def attend_kernel(blocks, factor, bias_ref, own_q_ref, far_q_ref, *refs):
    kv_refs = refs[:blocks]
    own_acc_ref, own_stat_ref, code_ref = refs[blocks : blocks + 3]
    scratch = refs[blocks + 3 :]
    heads, rows, width = own_q_ref.shape
    span = kv_refs[0].shape[2]
    cubes = rows // CUBE
    lane = lax.broadcasted_iota(jnp.int32, (rows, width), 1)
    ones = jnp.ones((span, width), jnp.bfloat16)
    for head in range(heads):
        for half, q_ref in enumerate((own_q_ref, far_q_ref)):
            score_ref = scratch[(2 * head + half) % len(scratch)]
            cube = lax.broadcasted_iota(jnp.int32, (rows, width), 0) // CUBE + half * cubes
            query = jnp.concatenate([q_ref[head], (lane == cube).astype(jnp.bfloat16)], axis=1)
            top = jnp.full((rows, width), NEG, jnp.float32)
            for b, ref in enumerate(kv_refs):
                key = jnp.concatenate([ref[0, head], bias_ref[b * span : (b + 1) * span]], axis=1)
                scores = lax.dot_general(
                    query, key, (((1,), (1,)), ((), ())), preferred_element_type=jnp.float32
                )
                for i in range(0, span, width):
                    top = jnp.maximum(top, scores[:, i : i + width])
                score_ref[:, b * span : (b + 1) * span] = scores
            top = jnp.max(top, axis=1, keepdims=True)
            both = jnp.zeros((rows, 2 * width), jnp.float32)
            for b, ref in enumerate(kv_refs):
                listed = jnp.concatenate([ref[1, head], ones], axis=1)
                weights = jnp.exp2((score_ref[:, b * span : (b + 1) * span] - top) * factor)
                both += jnp.dot(
                    weights.astype(jnp.bfloat16), listed, preferred_element_type=jnp.float32
                )
            acc, total = both[:, :width], both[:, width:]
            level = jnp.maximum(top * factor, -30000.0) + jnp.log2(total)
            result = acc / total
            if half == 0:
                own_acc_ref[head] = result
                own_stat_ref[head] = jnp.transpose(level)[:8]
            else:
                peak = jnp.max(jnp.abs(result), axis=1, keepdims=True)
                power = jnp.ceil(jnp.log2(jnp.maximum(peak, 1e-30)) + 1e-3)
                code = jnp.floor(result * (jnp.exp2(-power) * LEVELS) + 0.5)
                code_ref[head, :rows] = code.astype(jnp.int32).astype(jnp.int16)
                units = jnp.floor(level)
                fraction = jnp.floor((level - units) * FRACTION + 0.5)
                stats = jnp.where(lane == 0, units, jnp.where(lane == 1, fraction, power))
                stats = jnp.transpose(stats)[:8]
                stats = jnp.concatenate(
                    [stats[:, i * width : (i + 1) * width] for i in range(rows // width)], axis=0
                )
                code_ref[head, rows:] = stats.astype(jnp.int32).astype(jnp.int16)


def attend(heads, bias, own_q, far_q, blocks):
    span, width = blocks[0][1].shape[2:]
    rows = own_q[1].shape[1]
    factor = math.log2(math.e) / math.sqrt(width)
    extra = 8 * (rows // width)

    def whole(array):
        return pl.BlockSpec(array.shape, lambda h: (0,) * len(array.shape))

    def queries_from(start):
        shape = tuple(pl.Element(n) for n in (heads, rows, width))
        return pl.BlockSpec(shape, lambda h: (start, 0, 0))

    def block_from(start):
        shape = tuple(pl.Element(n) for n in (2, heads, span, width))
        return pl.BlockSpec(shape, lambda h: (0, start, 0, 0))

    outs = [
        jax.ShapeDtypeStruct((heads, rows, width), jnp.float32),
        jax.ShapeDtypeStruct((heads, 8, rows), jnp.float32),
        jax.ShapeDtypeStruct((heads, rows + extra, width), jnp.int16),
    ]
    work = heads * 2 * rows * len(blocks) * span
    return pl.pallas_call(
        functools.partial(attend_kernel, len(blocks), factor),
        grid=(1,),
        in_specs=[whole(bias), queries_from(own_q[0]), queries_from(far_q[0])]
        + [block_from(start) for start, _ in blocks],
        out_specs=[whole(out) for out in outs],
        out_shape=outs,
        scratch_shapes=[pltpu.VMEM((rows, len(blocks) * span), jnp.float32)] * 4,
        compiler_params=pltpu.CompilerParams(vmem_limit_bytes=60 * 1024 * 1024),
        cost_estimate=pl.CostEstimate(
            flops=work * width * 8,
            bytes_accessed=heads * rows * width * 2 * (2 * len(blocks) + 5),
            transcendentals=work,
        ),
    )(bias, own_q[1], far_q[1], *[array for _, array in blocks])


def merge_kernel(own_acc_ref, own_stat_ref, code_ref, gate_ref, coarse_ref, *out_refs):
    tokens = out_refs[0].shape[1]
    heads, rows, width = own_acc_ref.shape
    for head in range(heads):
        stats = code_ref[head, rows:].astype(jnp.int32).astype(jnp.float32)
        for i in range(rows // width):
            part = slice(i * width, (i + 1) * width)
            sent = stats[8 * i : 8 * i + 8]
            own = own_stat_ref[head, :, part]
            far = sent[0:1] + sent[1:2] * (1.0 / FRACTION)
            far = jnp.broadcast_to(far, own.shape)
            best = jnp.maximum(own, far)
            own = jnp.exp2(own - best)
            far = jnp.exp2(far - best)
            total = own + far
            step = jnp.exp2(jnp.broadcast_to(sent[2:3], own.shape)) * (1.0 / LEVELS)
            gate = jnp.broadcast_to(gate_ref[head, :, part].astype(jnp.float32), own.shape)
            row = lax.broadcasted_iota(jnp.int32, own.shape, 0)
            shares = jnp.where(row == 0, own / total, jnp.where(row == 1, far / total * step, gate))
            shares = jnp.transpose(shares)
            code = code_ref[head, part].astype(jnp.int32).astype(jnp.float32)
            fine = own_acc_ref[head, part] * shares[:, 0:1] + code * shares[:, 1:2]
            per = width // CUBE
            coarse = jnp.concatenate(
                [
                    jnp.broadcast_to(coarse_ref[head, c : c + 1], (CUBE, width))
                    for c in range(i * per, (i + 1) * per)
                ],
                axis=0,
            )
            at = i * width % tokens
            out_refs[i * width // tokens][head, at : at + width] = (fine + shares[:, 2:3] * coarse).astype(jnp.bfloat16)


def merge(first, tokens, own_acc, own_stat, code, gate, coarse):
    heads, rows, width = own_acc.shape

    def block(array, start):
        shape = (heads,) + array.shape[1:]
        return pl.BlockSpec(tuple(pl.Element(n) for n in shape), lambda h: (start, 0, 0))

    arrays = [own_acc, own_stat, code, gate, coarse]
    outs = [jax.ShapeDtypeStruct((heads, tokens, width), jnp.bfloat16)] * (rows // tokens)
    return pl.pallas_call(
        merge_kernel,
        grid=(1,),
        in_specs=[block(a, s) for a, s in zip(arrays, (0, 0, 0, first, first))],
        out_specs=[block(out, 0) for out in outs],
        out_shape=outs,
        compiler_params=pltpu.CompilerParams(vmem_limit_bytes=16 * 1024 * 1024),
        cost_estimate=pl.CostEstimate(
            flops=heads * rows * width * 4, bytes_accessed=heads * rows * width * 8, transcendentals=0
        ),
    )(*arrays)


def after(array, *others):
    return lax.optimization_barrier((array,) + others)[0] if others else array


def plan_of(heads):
    if heads == 6:
        return [2, 2, 1, 1], [(0, 2), (2, 4)], [(0, 1), (1, 2), (2, 4)], [(0, 1), (1, 4)]
    return [heads], [(0, 1)], [(0, 1)], [(0, 1)]


def body(ring, queries, keys, values, block_lists, coarse_gate):
    tokens, width = queries.shape[1:]
    scale = 1.0 / math.sqrt(width)
    half = ring // 2
    me = lax.axis_index("ctx")

    def swap(array, bit):
        return lax.ppermute(array, "ctx", [(i, i ^ bit) for i in range(ring)])

    split = queries.shape[0] % 2 == 0
    offsets = [0, 1] if split else [0]
    heads = queries.shape[0] // len(offsets)
    own_cubes = tokens // CUBE
    sizes, to_side, to_next, to_far = plan_of(heads)
    starts = [sum(sizes[:i]) for i in range(len(sizes) + 1)]
    parts = range(len(sizes))
    spans = [(starts[low], starts[high] - starts[low]) for low, high in to_side + to_next]

    def cut(array, start):
        return lax.dynamic_slice_in_dim(array, start, heads, 0)

    pooled = jnp.concatenate([pool_cubes(keys), pool_cubes(values)], axis=2)
    lists = jnp.zeros((1, own_cubes + 1, 2 * width), jnp.bfloat16)
    lists = lists.at[0, :own_cubes, : block_lists.shape[1]].set(block_lists.astype(jnp.bfloat16))
    gate = coarse_gate.reshape(-1, 1, 2 * width)
    small = jnp.concatenate([jnp.concatenate([pooled, gate], axis=1), lists], axis=0)
    far_small = swap(small, half)
    small = [small, far_small]
    if split:
        core = me & 1
        mine, theirs = core * heads, (1 - core) * heads
        got = swap(jnp.stack([cut(keys, theirs), cut(values, theirs)]), 1)
        packs = pack_groups(spans, core, keys, values, got)
        queries = after(queries, packs[0])
        queries = jnp.concatenate([cut(queries, mine), swap(cut(queries, theirs), 1)], axis=1)
        both = jnp.concatenate(small, axis=1)
        got = swap(jnp.concatenate([cut(both, theirs), both[-1:]], axis=0), 1)
        both = jnp.concatenate([cut(both, mine), both[-1:]], axis=0)
        step = own_cubes + 1
        small = [both[:, :step], got[:, :step], both[:, step:], got[:, step:]]
    else:
        packs = [jnp.stack([keys[f : f + n], values[f : f + n]]) for f, n in spans]
    pooled = jnp.concatenate([part[:heads, :own_cubes] for part in small], axis=1)
    lists = jnp.concatenate([part[heads, :own_cubes] for part in small], axis=0)
    lists = lists[:, : block_lists.shape[1]].astype(jnp.int32)
    gate = jnp.concatenate([part[:heads, own_cubes:] for part in small[: len(offsets)]], axis=2)
    heads, rows, width = queries.shape
    cubes = rows // CUBE
    side = len(offsets)
    masks = list(range(0, half, side))
    hops = [m for m in masks[1:] if m & -m == m]
    pooled_q = pool_cubes(queries)

    lanes = jnp.concatenate(
        [
            (me ^ m ^ o) * own_cubes + jnp.arange(tokens, dtype=jnp.int32) // CUBE
            for m in masks
            for o in offsets
        ]
    )
    hit = jnp.any(lists[:, :, None] == lanes[None, None, :], axis=1)
    bias = jnp.where(hit, 0.0, NEG).astype(jnp.bfloat16)
    bias = jnp.pad(bias.T, ((0, 0), (0, width - 2 * cubes)))

    side_packs, next_packs = packs[: len(to_side)], packs[len(to_side) :]
    held = [{} for _ in parts]
    wait = [far_small]
    for (low, high), pack in zip(to_side, side_packs):
        got = swap(after(pack, *wait), side)
        for part in range(low, high):
            held[part][0] = (starts[part] - starts[low], pack)
            held[part][side] = (starts[part] - starts[low], got)
        wait = [got]
    others = [far_small]
    pooled_wait = [far_small]
    wait = [far_small]
    for (low, high), pack in zip(to_next, next_packs):
        for mask in hops[1:]:
            got = swap(after(pack, *wait), mask)
            for part in range(low, high):
                held[part][mask] = (starts[part] - starts[low], got)
        if low == 0:
            others = [got]
        wait = [got]
    far_q = []
    wait = others
    for low, high in to_far:
        got = swap(after(queries[starts[low] : starts[high]], *wait), half)
        far_q += [(starts[part] - starts[low], got) for part in range(low, high)]
        wait = [got]
    for bit in hops:
        other = swap(after(pooled, *pooled_wait), bit)
        pooled = jnp.concatenate([pooled, other], axis=1)
        pooled_wait = others
    done = []
    for part in parts:
        wait = []
        if part == 1:
            bias = after(bias, held[parts[-1]][side][1])
        if part >= 2:
            wait = [done[part - 2][0]]
        if part == 2:
            bias = after(bias, done[0][2])
        for mask in masks[1:]:
            bit = mask & -mask
            if mask != bit:
                start, array = held[part][mask ^ bit]
                if array.shape[1] != sizes[part]:
                    array = array[:, start : start + sizes[part]]
                held[part][mask] = (0, swap(after(array, *wait), bit))
        blocks = [held[part][mask] for mask in masks]
        own_acc, own_stat, code = attend(
            sizes[part], bias, (starts[part], queries), far_q[part], blocks
        )
        done.append((own_acc, own_stat, swap(code, half)))

    coarse_scores = (
        jnp.einsum(
            "hqd,hkd->hqk", pooled_q, pooled[..., :width], preferred_element_type=jnp.float32
        )
        * scale
    )
    coarse_top = jnp.max(coarse_scores, axis=-1, keepdims=True)
    coarse_weights = jnp.exp(coarse_scores - coarse_top).astype(jnp.bfloat16)
    coarse_total = jnp.sum(coarse_weights.astype(jnp.float32), axis=-1)
    coarse_cube = (
        jnp.einsum(
            "hqk,hkd->hqd", coarse_weights, pooled[..., width:], preferred_element_type=jnp.float32
        )
        / coarse_total[..., None]
    )
    kept, received = [], []
    for part in parts:
        own_acc, own_stat, code = done[part]
        if part != parts[-1]:
            code = after(code, done[parts[-1]][0])
        outs = merge(starts[part], tokens, own_acc, own_stat, code, gate, coarse_cube)
        kept.append(outs[0])
        if split:
            received.append(swap(outs[1], 1))
    kept = jnp.concatenate(kept, axis=0)
    if not split:
        return kept
    received = jnp.concatenate(received, axis=0)
    first = jnp.where(core == 0, kept, received)
    second = jnp.where(core == 0, received, kept)
    return jnp.concatenate([first, second], axis=0)


def solution(mesh):
    in_specs = (
        P("head", "ctx", None),
        P("head", "ctx", None),
        P("head", "ctx", None),
        P("ctx", None),
        P("head", "ctx"),
    )
    out_specs = P("head", "ctx", None)
    return jax.shard_map(
        functools.partial(body, mesh.shape["ctx"]),
        mesh=mesh,
        in_specs=in_specs,
        out_specs=out_specs,
        check_vma=False,
    )
```

```python
import functools
import math

import jax
import jax.numpy as jnp
from jax import lax
from jax.experimental import pallas as pl
from jax.experimental.pallas import tpu as pltpu
from jax.sharding import PartitionSpec as P

CUBE = 64
NEG = -1e30
LEVELS = 32766.0
FRACTION = 32767.0


def pool_cubes(field):
    heads, tokens, width = field.shape
    summed = jnp.sum(field.reshape(heads, tokens // CUBE, CUBE, width), axis=2, dtype=jnp.float32)
    return (summed / CUBE).astype(jnp.bfloat16)


def pack_kernel(spans, core_ref, keys_ref, values_ref, got_ref, *pack_refs):
    tokens = keys_ref.shape[1]
    share = got_ref.shape[1]
    for (first, size), pack_ref in zip(spans, pack_refs):
        heads = pl.ds(core_ref[0] * share + first, size)
        pack_ref[0, :, :tokens] = keys_ref[heads]
        pack_ref[1, :, :tokens] = values_ref[heads]
        pack_ref[:, :, tokens:] = got_ref[:, first : first + size]


def pack_groups(spans, core, keys, values, got):
    tokens, width = keys.shape[1:]

    def whole(shape):
        return pl.BlockSpec(tuple(shape), lambda h, core: (0,) * len(shape))

    outs = [jax.ShapeDtypeStruct((2, size, 2 * tokens, width), keys.dtype) for _, size in spans]
    return pl.pallas_call(
        functools.partial(pack_kernel, spans),
        grid_spec=pltpu.PrefetchScalarGridSpec(
            num_scalar_prefetch=1,
            grid=(1,),
            in_specs=[whole(a.shape) for a in (keys, values, got)],
            out_specs=[whole(out.shape) for out in outs],
        ),
        out_shape=outs,
        compiler_params=pltpu.CompilerParams(vmem_limit_bytes=24 * 1024 * 1024),
    )(core[None], keys, values, got)


def attend_kernel(blocks, factor, bias_ref, own_q_ref, far_q_ref, *refs):
    kv_refs = refs[:blocks]
    own_acc_ref, own_stat_ref, code_ref = refs[blocks : blocks + 3]
    scratch = refs[blocks + 3 :]
    heads, rows, width = own_q_ref.shape
    span = kv_refs[0].shape[2]
    cubes = rows // CUBE
    lane = lax.broadcasted_iota(jnp.int32, (rows, width), 1)
    ones = jnp.ones((span, width), jnp.bfloat16)
    for head in range(heads):
        for half, q_ref in enumerate((own_q_ref, far_q_ref)):
            score_ref = scratch[(2 * head + half) % len(scratch)]
            cube = lax.broadcasted_iota(jnp.int32, (rows, width), 0) // CUBE + half * cubes
            query = jnp.concatenate([q_ref[head], (lane == cube).astype(jnp.bfloat16)], axis=1)
            top = jnp.full((rows, width), NEG, jnp.float32)
            for b, ref in enumerate(kv_refs):
                key = jnp.concatenate([ref[0, head], bias_ref[b * span : (b + 1) * span]], axis=1)
                scores = lax.dot_general(
                    query, key, (((1,), (1,)), ((), ())), preferred_element_type=jnp.float32
                )
                for i in range(0, span, width):
                    top = jnp.maximum(top, scores[:, i : i + width])
                score_ref[:, b * span : (b + 1) * span] = scores
            top = jnp.max(top, axis=1, keepdims=True)
            both = jnp.zeros((rows, 2 * width), jnp.float32)
            for b, ref in enumerate(kv_refs):
                listed = jnp.concatenate([ref[1, head], ones], axis=1)
                weights = jnp.exp2((score_ref[:, b * span : (b + 1) * span] - top) * factor)
                both += jnp.dot(
                    weights.astype(jnp.bfloat16), listed, preferred_element_type=jnp.float32
                )
            acc, total = both[:, :width], both[:, width:]
            level = jnp.maximum(top * factor, -30000.0) + jnp.log2(total)
            result = acc / total
            if half == 0:
                own_acc_ref[head] = result
                own_stat_ref[head] = jnp.transpose(level)[:8]
            else:
                peak = jnp.max(jnp.abs(result), axis=1, keepdims=True)
                power = jnp.ceil(jnp.log2(jnp.maximum(peak, 1e-30)) + 1e-3)
                code = jnp.floor(result * (jnp.exp2(-power) * LEVELS) + 0.5)
                code_ref[head, :rows] = code.astype(jnp.int32).astype(jnp.int16)
                units = jnp.floor(level)
                fraction = jnp.floor((level - units) * FRACTION + 0.5)
                stats = jnp.where(lane == 0, units, jnp.where(lane == 1, fraction, power))
                stats = jnp.transpose(stats)[:8]
                stats = jnp.concatenate(
                    [stats[:, i * width : (i + 1) * width] for i in range(rows // width)], axis=0
                )
                code_ref[head, rows:] = stats.astype(jnp.int32).astype(jnp.int16)


def attend(heads, bias, own_q, far_q, blocks):
    span, width = blocks[0][1].shape[2:]
    rows = own_q[1].shape[1]
    factor = math.log2(math.e) / math.sqrt(width)
    extra = 8 * (rows // width)

    def whole(array):
        return pl.BlockSpec(array.shape, lambda h: (0,) * len(array.shape))

    def queries_from(start):
        shape = tuple(pl.Element(n) for n in (heads, rows, width))
        return pl.BlockSpec(shape, lambda h: (start, 0, 0))

    def block_from(start):
        shape = tuple(pl.Element(n) for n in (2, heads, span, width))
        return pl.BlockSpec(shape, lambda h: (0, start, 0, 0))

    outs = [
        jax.ShapeDtypeStruct((heads, rows, width), jnp.float32),
        jax.ShapeDtypeStruct((heads, 8, rows), jnp.float32),
        jax.ShapeDtypeStruct((heads, rows + extra, width), jnp.int16),
    ]
    work = heads * 2 * rows * len(blocks) * span
    return pl.pallas_call(
        functools.partial(attend_kernel, len(blocks), factor),
        grid=(1,),
        in_specs=[whole(bias), queries_from(own_q[0]), queries_from(far_q[0])]
        + [block_from(start) for start, _ in blocks],
        out_specs=[whole(out) for out in outs],
        out_shape=outs,
        scratch_shapes=[pltpu.VMEM((rows, len(blocks) * span), jnp.float32)] * 4,
        compiler_params=pltpu.CompilerParams(vmem_limit_bytes=(38 if len(blocks) < 8 else 60) * 1024 * 1024),
        cost_estimate=pl.CostEstimate(
            flops=work * width * 8,
            bytes_accessed=heads * rows * width * 2 * (2 * len(blocks) + 5),
            transcendentals=work,
        ),
    )(bias, own_q[1], far_q[1], *[array for _, array in blocks])


def merge_kernel(own_acc_ref, own_stat_ref, code_ref, gate_ref, coarse_ref, *out_refs):
    tokens = out_refs[0].shape[1]
    heads, rows, width = own_acc_ref.shape
    for head in range(heads):
        stats = code_ref[head, rows:].astype(jnp.int32).astype(jnp.float32)
        for i in range(rows // width):
            part = slice(i * width, (i + 1) * width)
            sent = stats[8 * i : 8 * i + 8]
            own = own_stat_ref[head, :, part]
            far = sent[0:1] + sent[1:2] * (1.0 / FRACTION)
            far = jnp.broadcast_to(far, own.shape)
            best = jnp.maximum(own, far)
            own = jnp.exp2(own - best)
            far = jnp.exp2(far - best)
            total = own + far
            step = jnp.exp2(jnp.broadcast_to(sent[2:3], own.shape)) * (1.0 / LEVELS)
            gate = jnp.broadcast_to(gate_ref[head, :, part].astype(jnp.float32), own.shape)
            row = lax.broadcasted_iota(jnp.int32, own.shape, 0)
            shares = jnp.where(row == 0, own / total, jnp.where(row == 1, far / total * step, gate))
            shares = jnp.transpose(shares)
            code = code_ref[head, part].astype(jnp.int32).astype(jnp.float32)
            fine = own_acc_ref[head, part] * shares[:, 0:1] + code * shares[:, 1:2]
            per = width // CUBE
            coarse = jnp.concatenate(
                [
                    jnp.broadcast_to(coarse_ref[head, c : c + 1], (CUBE, width))
                    for c in range(i * per, (i + 1) * per)
                ],
                axis=0,
            )
            at = i * width % tokens
            out_refs[i * width // tokens][head, at : at + width] = (fine + shares[:, 2:3] * coarse).astype(jnp.bfloat16)


def merge(first, tokens, own_acc, own_stat, code, gate, coarse):
    heads, rows, width = own_acc.shape

    def block(array, start):
        shape = (heads,) + array.shape[1:]
        return pl.BlockSpec(tuple(pl.Element(n) for n in shape), lambda h: (start, 0, 0))

    arrays = [own_acc, own_stat, code, gate, coarse]
    outs = [jax.ShapeDtypeStruct((heads, tokens, width), jnp.bfloat16)] * (rows // tokens)
    return pl.pallas_call(
        merge_kernel,
        grid=(1,),
        in_specs=[block(a, s) for a, s in zip(arrays, (0, 0, 0, first, first))],
        out_specs=[block(out, 0) for out in outs],
        out_shape=outs,
        compiler_params=pltpu.CompilerParams(vmem_limit_bytes=16 * 1024 * 1024),
        cost_estimate=pl.CostEstimate(
            flops=heads * rows * width * 4, bytes_accessed=heads * rows * width * 8, transcendentals=0
        ),
    )(*arrays)


def after(array, *others):
    return lax.optimization_barrier((array,) + others)[0] if others else array


def plan_of(heads):
    if heads == 6:
        return [2, 2, 1, 1], [(0, 2), (2, 4)], [(0, 1), (1, 2), (2, 4)], [(0, 1), (1, 4)]
    return [heads], [(0, 1)], [(0, 1)], [(0, 1)]


def body(ring, queries, keys, values, block_lists, coarse_gate):
    tokens, width = queries.shape[1:]
    scale = 1.0 / math.sqrt(width)
    half = ring // 2
    me = lax.axis_index("ctx")

    def swap(array, bit):
        return lax.ppermute(array, "ctx", [(i, i ^ bit) for i in range(ring)])

    split = queries.shape[0] % 2 == 0
    offsets = [0, 1] if split else [0]
    heads = queries.shape[0] // len(offsets)
    own_cubes = tokens // CUBE
    sizes, to_side, to_next, to_far = plan_of(heads)
    starts = [sum(sizes[:i]) for i in range(len(sizes) + 1)]
    parts = range(len(sizes))
    spans = [(starts[low], starts[high] - starts[low]) for low, high in to_side + to_next]

    def cut(array, start):
        return lax.dynamic_slice_in_dim(array, start, heads, 0)

    pooled = jnp.concatenate([pool_cubes(keys), pool_cubes(values)], axis=2)
    lists = jnp.zeros((1, own_cubes + 1, 2 * width), jnp.bfloat16)
    lists = lists.at[0, :own_cubes, : block_lists.shape[1]].set(block_lists.astype(jnp.bfloat16))
    gate = coarse_gate.reshape(-1, 1, 2 * width)
    small = jnp.concatenate([jnp.concatenate([pooled, gate], axis=1), lists], axis=0)
    far_small = swap(small, half)
    small = [small, far_small]
    if split:
        core = me & 1
        mine, theirs = core * heads, (1 - core) * heads
        got = swap(jnp.stack([cut(keys, theirs), cut(values, theirs)]), 1)
        packs = pack_groups(spans, core, keys, values, got)
        queries = after(queries, packs[0])
        queries = jnp.concatenate([cut(queries, mine), swap(cut(queries, theirs), 1)], axis=1)
        both = jnp.concatenate(small, axis=1)
        got = swap(jnp.concatenate([cut(both, theirs), both[-1:]], axis=0), 1)
        both = jnp.concatenate([cut(both, mine), both[-1:]], axis=0)
        step = own_cubes + 1
        small = [both[:, :step], got[:, :step], both[:, step:], got[:, step:]]
    else:
        packs = [jnp.stack([keys[f : f + n], values[f : f + n]]) for f, n in spans]
    pooled = jnp.concatenate([part[:heads, :own_cubes] for part in small], axis=1)
    lists = jnp.concatenate([part[heads, :own_cubes] for part in small], axis=0)
    lists = lists[:, : block_lists.shape[1]].astype(jnp.int32)
    gate = jnp.concatenate([part[:heads, own_cubes:] for part in small[: len(offsets)]], axis=2)
    heads, rows, width = queries.shape
    cubes = rows // CUBE
    side = len(offsets)
    masks = list(range(0, half, side))
    hops = [m for m in masks[1:] if m & -m == m]
    pooled_q = pool_cubes(queries)

    lanes = jnp.concatenate(
        [
            (me ^ m ^ o) * own_cubes + jnp.arange(tokens, dtype=jnp.int32) // CUBE
            for m in masks
            for o in offsets
        ]
    )
    hit = jnp.any(lists[:, :, None] == lanes[None, None, :], axis=1)
    bias = jnp.where(hit, 0.0, NEG).astype(jnp.bfloat16)
    bias = jnp.pad(bias.T, ((0, 0), (0, width - 2 * cubes)))

    side_packs, next_packs = packs[: len(to_side)], packs[len(to_side) :]
    held = [{} for _ in parts]
    wait = [far_small]
    for (low, high), pack in zip(to_side, side_packs):
        got = swap(after(pack, *wait), side)
        for part in range(low, high):
            held[part][0] = (starts[part] - starts[low], pack)
            held[part][side] = (starts[part] - starts[low], got)
        wait = [got]
    others = [far_small]
    pooled_wait = [far_small]
    wait = [far_small]
    for (low, high), pack in zip(to_next, next_packs):
        for mask in hops[1:]:
            got = swap(after(pack, *wait), mask)
            for part in range(low, high):
                held[part][mask] = (starts[part] - starts[low], got)
        if low == 0:
            others = [got]
        wait = [got]
    far_q = []
    wait = others
    for low, high in to_far:
        got = swap(after(queries[starts[low] : starts[high]], *wait), half)
        far_q += [(starts[part] - starts[low], got) for part in range(low, high)]
    for bit in hops:
        other = swap(after(pooled, *pooled_wait), bit)
        pooled = jnp.concatenate([pooled, other], axis=1)
        pooled_wait = others
    done = []
    for part in parts:
        wait = []
        if part == 1:
            bias = after(bias, held[parts[-1]][side][1])
        if part >= 2:
            wait = [done[part - 2][0]]
        if part == 2:
            bias = after(bias, done[0][2])
        for mask in masks[1:]:
            bit = mask & -mask
            if mask != bit:
                start, array = held[part][mask ^ bit]
                if array.shape[1] != sizes[part]:
                    array = array[:, start : start + sizes[part]]
                held[part][mask] = (0, swap(after(array, *wait), bit))
        blocks = [held[part][mask] for mask in masks]
        own_acc, own_stat, code = attend(
            sizes[part], bias, (starts[part], queries), far_q[part], blocks
        )
        done.append((own_acc, own_stat, swap(code, half)))

    coarse_scores = (
        jnp.einsum(
            "hqd,hkd->hqk", pooled_q, pooled[..., :width], preferred_element_type=jnp.float32
        )
        * scale
    )
    coarse_top = jnp.max(coarse_scores, axis=-1, keepdims=True)
    coarse_weights = jnp.exp(coarse_scores - coarse_top).astype(jnp.bfloat16)
    coarse_total = jnp.sum(coarse_weights.astype(jnp.float32), axis=-1)
    coarse_cube = (
        jnp.einsum(
            "hqk,hkd->hqd", coarse_weights, pooled[..., width:], preferred_element_type=jnp.float32
        )
        / coarse_total[..., None]
    )
    kept, received = [], []
    for part in parts:
        own_acc, own_stat, code = done[part]
        if part != parts[-1]:
            code = after(code, done[parts[-1]][0])
        outs = merge(starts[part], tokens, own_acc, own_stat, code, gate, coarse_cube)
        kept.append(outs[0])
        if split:
            received.append(swap(outs[1], 1))
    kept = jnp.concatenate(kept, axis=0)
    if not split:
        return kept
    received = jnp.concatenate(received, axis=0)
    first = jnp.where(core == 0, kept, received)
    second = jnp.where(core == 0, received, kept)
    return jnp.concatenate([first, second], axis=0)


def solution(mesh):
    in_specs = (
        P("head", "ctx", None),
        P("head", "ctx", None),
        P("head", "ctx", None),
        P("ctx", None),
        P("head", "ctx"),
    )
    out_specs = P("head", "ctx", None)
    return jax.shard_map(
        functools.partial(body, mesh.shape["ctx"]),
        mesh=mesh,
        in_specs=in_specs,
        out_specs=out_specs,
        check_vma=False,
    )
```

```python
import functools
import math

import jax
import jax.numpy as jnp
from jax import lax
from jax.experimental import pallas as pl
from jax.experimental.pallas import tpu as pltpu
from jax.sharding import PartitionSpec as P

CUBE = 64
NEG = -1e30
LEVELS = 32766.0
FRACTION = 32767.0


def pool_cubes(field):
    heads, tokens, width = field.shape
    summed = jnp.sum(field.reshape(heads, tokens // CUBE, CUBE, width), axis=2, dtype=jnp.float32)
    return (summed / CUBE).astype(jnp.bfloat16)


def pack_kernel(spans, core_ref, keys_ref, values_ref, got_ref, *pack_refs):
    tokens = keys_ref.shape[1]
    share = got_ref.shape[1]
    for (first, size), pack_ref in zip(spans, pack_refs):
        heads = pl.ds(core_ref[0] * share + first, size)
        pack_ref[0, :, :tokens] = keys_ref[heads]
        pack_ref[1, :, :tokens] = values_ref[heads]
        pack_ref[:, :, tokens:] = got_ref[:, first : first + size]


def pack_groups(spans, core, keys, values, got):
    tokens, width = keys.shape[1:]

    def whole(shape):
        return pl.BlockSpec(tuple(shape), lambda h, core: (0,) * len(shape))

    outs = [jax.ShapeDtypeStruct((2, size, 2 * tokens, width), keys.dtype) for _, size in spans]
    return pl.pallas_call(
        functools.partial(pack_kernel, spans),
        grid_spec=pltpu.PrefetchScalarGridSpec(
            num_scalar_prefetch=1,
            grid=(1,),
            in_specs=[whole(a.shape) for a in (keys, values, got)],
            out_specs=[whole(out.shape) for out in outs],
        ),
        out_shape=outs,
        compiler_params=pltpu.CompilerParams(vmem_limit_bytes=24 * 1024 * 1024),
    )(core[None], keys, values, got)


def attend_kernel(blocks, factor, bias_ref, own_q_ref, far_q_ref, *refs):
    kv_refs = refs[:blocks]
    own_acc_ref, own_stat_ref, code_ref = refs[blocks : blocks + 3]
    scratch = refs[blocks + 3 :]
    heads, rows, width = own_q_ref.shape
    span = kv_refs[0].shape[2]
    cubes = rows // CUBE
    lane = lax.broadcasted_iota(jnp.int32, (rows, width), 1)
    ones = jnp.ones((span, width), jnp.bfloat16)
    for head in range(heads):
        for half, q_ref in enumerate((own_q_ref, far_q_ref)):
            score_ref = scratch[(2 * head + half) % len(scratch)]
            cube = lax.broadcasted_iota(jnp.int32, (rows, width), 0) // CUBE + half * cubes
            query = jnp.concatenate([q_ref[head], (lane == cube).astype(jnp.bfloat16)], axis=1)
            top = jnp.full((rows, width), NEG, jnp.float32)
            for b, ref in enumerate(kv_refs):
                key = jnp.concatenate([ref[0, head], bias_ref[b * span : (b + 1) * span]], axis=1)
                scores = lax.dot_general(
                    query, key, (((1,), (1,)), ((), ())), preferred_element_type=jnp.float32
                )
                for i in range(0, span, width):
                    top = jnp.maximum(top, scores[:, i : i + width])
                score_ref[:, b * span : (b + 1) * span] = scores
            top = jnp.max(top, axis=1, keepdims=True)
            both = jnp.zeros((rows, 2 * width), jnp.float32)
            for b, ref in enumerate(kv_refs):
                listed = jnp.concatenate([ref[1, head], ones], axis=1)
                weights = jnp.exp2((score_ref[:, b * span : (b + 1) * span] - top) * factor)
                both += jnp.dot(
                    weights.astype(jnp.bfloat16), listed, preferred_element_type=jnp.float32
                )
            acc, total = both[:, :width], both[:, width:]
            level = jnp.maximum(top * factor, -30000.0) + jnp.log2(total)
            result = acc / total
            if half == 0:
                own_acc_ref[head] = result
                own_stat_ref[head] = jnp.transpose(level)[:8]
            else:
                peak = jnp.max(jnp.abs(result), axis=1, keepdims=True)
                power = jnp.ceil(jnp.log2(jnp.maximum(peak, 1e-30)) + 1e-3)
                code = jnp.floor(result * (jnp.exp2(-power) * LEVELS) + 0.5)
                code_ref[head, :rows] = code.astype(jnp.int32).astype(jnp.int16)
                units = jnp.floor(level)
                fraction = jnp.floor((level - units) * FRACTION + 0.5)
                stats = jnp.where(lane == 0, units, jnp.where(lane == 1, fraction, power))
                stats = jnp.transpose(stats)[:8]
                stats = jnp.concatenate(
                    [stats[:, i * width : (i + 1) * width] for i in range(rows // width)], axis=0
                )
                code_ref[head, rows:] = stats.astype(jnp.int32).astype(jnp.int16)


def attend(heads, bias, own_q, far_q, blocks):
    span, width = blocks[0][1].shape[2:]
    rows = own_q[1].shape[1]
    factor = math.log2(math.e) / math.sqrt(width)
    extra = 8 * (rows // width)

    def whole(array):
        return pl.BlockSpec(array.shape, lambda h: (0,) * len(array.shape))

    def queries_from(start):
        shape = tuple(pl.Element(n) for n in (heads, rows, width))
        return pl.BlockSpec(shape, lambda h: (start, 0, 0))

    def block_from(start):
        shape = tuple(pl.Element(n) for n in (2, heads, span, width))
        return pl.BlockSpec(shape, lambda h: (0, start, 0, 0))

    outs = [
        jax.ShapeDtypeStruct((heads, rows, width), jnp.float32),
        jax.ShapeDtypeStruct((heads, 8, rows), jnp.float32),
        jax.ShapeDtypeStruct((heads, rows + extra, width), jnp.int16),
    ]
    work = heads * 2 * rows * len(blocks) * span
    return pl.pallas_call(
        functools.partial(attend_kernel, len(blocks), factor),
        grid=(1,),
        in_specs=[whole(bias), queries_from(own_q[0]), queries_from(far_q[0])]
        + [block_from(start) for start, _ in blocks],
        out_specs=[whole(out) for out in outs],
        out_shape=outs,
        scratch_shapes=[pltpu.VMEM((rows, len(blocks) * span), jnp.float32)] * 2,
        compiler_params=pltpu.CompilerParams(vmem_limit_bytes=(28 if len(blocks) < 8 else 60) * 1024 * 1024),
        cost_estimate=pl.CostEstimate(
            flops=work * width * 8,
            bytes_accessed=heads * rows * width * 2 * (2 * len(blocks) + 5),
            transcendentals=work,
        ),
    )(bias, own_q[1], far_q[1], *[array for _, array in blocks])


def merge_kernel(own_acc_ref, own_stat_ref, code_ref, gate_ref, coarse_ref, *out_refs):
    tokens = out_refs[0].shape[1]
    heads, rows, width = own_acc_ref.shape
    for head in range(heads):
        stats = code_ref[head, rows:].astype(jnp.int32).astype(jnp.float32)
        for i in range(rows // width):
            part = slice(i * width, (i + 1) * width)
            sent = stats[8 * i : 8 * i + 8]
            own = own_stat_ref[head, :, part]
            far = sent[0:1] + sent[1:2] * (1.0 / FRACTION)
            far = jnp.broadcast_to(far, own.shape)
            best = jnp.maximum(own, far)
            own = jnp.exp2(own - best)
            far = jnp.exp2(far - best)
            total = own + far
            step = jnp.exp2(jnp.broadcast_to(sent[2:3], own.shape)) * (1.0 / LEVELS)
            gate = jnp.broadcast_to(gate_ref[head, :, part].astype(jnp.float32), own.shape)
            row = lax.broadcasted_iota(jnp.int32, own.shape, 0)
            shares = jnp.where(row == 0, own / total, jnp.where(row == 1, far / total * step, gate))
            shares = jnp.transpose(shares)
            code = code_ref[head, part].astype(jnp.int32).astype(jnp.float32)
            fine = own_acc_ref[head, part] * shares[:, 0:1] + code * shares[:, 1:2]
            per = width // CUBE
            coarse = jnp.concatenate(
                [
                    jnp.broadcast_to(coarse_ref[head, c : c + 1], (CUBE, width))
                    for c in range(i * per, (i + 1) * per)
                ],
                axis=0,
            )
            at = i * width % tokens
            out_refs[i * width // tokens][head, at : at + width] = (fine + shares[:, 2:3] * coarse).astype(jnp.bfloat16)


def merge(first, tokens, own_acc, own_stat, code, gate, coarse):
    heads, rows, width = own_acc.shape

    def block(array, start):
        shape = (heads,) + array.shape[1:]
        return pl.BlockSpec(tuple(pl.Element(n) for n in shape), lambda h: (start, 0, 0))

    arrays = [own_acc, own_stat, code, gate, coarse]
    outs = [jax.ShapeDtypeStruct((heads, tokens, width), jnp.bfloat16)] * (rows // tokens)
    return pl.pallas_call(
        merge_kernel,
        grid=(1,),
        in_specs=[block(a, s) for a, s in zip(arrays, (0, 0, 0, first, first))],
        out_specs=[block(out, 0) for out in outs],
        out_shape=outs,
        compiler_params=pltpu.CompilerParams(vmem_limit_bytes=16 * 1024 * 1024),
        cost_estimate=pl.CostEstimate(
            flops=heads * rows * width * 4, bytes_accessed=heads * rows * width * 8, transcendentals=0
        ),
    )(*arrays)


def after(array, *others):
    return lax.optimization_barrier((array,) + others)[0] if others else array


def plan_of(heads):
    if heads == 6:
        return [2, 2, 1, 1], [(0, 2), (2, 4)], [(0, 1), (1, 2), (2, 4)], [(0, 1), (1, 4)]
    return [heads], [(0, 1)], [(0, 1)], [(0, 1)]


def body(ring, queries, keys, values, block_lists, coarse_gate):
    tokens, width = queries.shape[1:]
    scale = 1.0 / math.sqrt(width)
    half = ring // 2
    me = lax.axis_index("ctx")

    def swap(array, bit):
        return lax.ppermute(array, "ctx", [(i, i ^ bit) for i in range(ring)])

    split = queries.shape[0] % 2 == 0
    offsets = [0, 1] if split else [0]
    heads = queries.shape[0] // len(offsets)
    own_cubes = tokens // CUBE
    sizes, to_side, to_next, to_far = plan_of(heads)
    starts = [sum(sizes[:i]) for i in range(len(sizes) + 1)]
    parts = range(len(sizes))
    spans = [(starts[low], starts[high] - starts[low]) for low, high in to_side + to_next]

    def cut(array, start):
        return lax.dynamic_slice_in_dim(array, start, heads, 0)

    pooled = jnp.concatenate([pool_cubes(keys), pool_cubes(values)], axis=2)
    lists = jnp.zeros((1, own_cubes + 1, 2 * width), jnp.bfloat16)
    lists = lists.at[0, :own_cubes, : block_lists.shape[1]].set(block_lists.astype(jnp.bfloat16))
    gate = coarse_gate.reshape(-1, 1, 2 * width)
    small = jnp.concatenate([jnp.concatenate([pooled, gate], axis=1), lists], axis=0)
    far_small = swap(small, half)
    small = [small, far_small]
    if split:
        core = me & 1
        mine, theirs = core * heads, (1 - core) * heads
        got = swap(jnp.stack([cut(keys, theirs), cut(values, theirs)]), 1)
        packs = pack_groups(spans, core, keys, values, got)
        queries = after(queries, packs[0])
        queries = jnp.concatenate([cut(queries, mine), swap(cut(queries, theirs), 1)], axis=1)
        both = jnp.concatenate(small, axis=1)
        got = swap(jnp.concatenate([cut(both, theirs), both[-1:]], axis=0), 1)
        both = jnp.concatenate([cut(both, mine), both[-1:]], axis=0)
        step = own_cubes + 1
        small = [both[:, :step], got[:, :step], both[:, step:], got[:, step:]]
    else:
        packs = [jnp.stack([keys[f : f + n], values[f : f + n]]) for f, n in spans]
    pooled = jnp.concatenate([part[:heads, :own_cubes] for part in small], axis=1)
    lists = jnp.concatenate([part[heads, :own_cubes] for part in small], axis=0)
    lists = lists[:, : block_lists.shape[1]].astype(jnp.int32)
    gate = jnp.concatenate([part[:heads, own_cubes:] for part in small[: len(offsets)]], axis=2)
    heads, rows, width = queries.shape
    cubes = rows // CUBE
    side = len(offsets)
    masks = list(range(0, half, side))
    hops = [m for m in masks[1:] if m & -m == m]
    pooled_q = pool_cubes(queries)

    lanes = jnp.concatenate(
        [
            (me ^ m ^ o) * own_cubes + jnp.arange(tokens, dtype=jnp.int32) // CUBE
            for m in masks
            for o in offsets
        ]
    )
    hit = jnp.any(lists[:, :, None] == lanes[None, None, :], axis=1)
    bias = jnp.where(hit, 0.0, NEG).astype(jnp.bfloat16)
    bias = jnp.pad(bias.T, ((0, 0), (0, width - 2 * cubes)))

    side_packs, next_packs = packs[: len(to_side)], packs[len(to_side) :]
    held = [{} for _ in parts]
    wait = [far_small]
    for (low, high), pack in zip(to_side, side_packs):
        got = swap(after(pack, *wait), side)
        for part in range(low, high):
            held[part][0] = (starts[part] - starts[low], pack)
            held[part][side] = (starts[part] - starts[low], got)
        wait = [got]
    others = [far_small]
    pooled_wait = [far_small]
    wait = [far_small]
    for (low, high), pack in zip(to_next, next_packs):
        for mask in hops[1:]:
            got = swap(after(pack, *wait), mask)
            for part in range(low, high):
                held[part][mask] = (starts[part] - starts[low], got)
        if low == 0:
            others = [got]
        wait = [got]
    far_q = []
    wait = others
    for low, high in to_far:
        got = swap(after(queries[starts[low] : starts[high]], *wait), half)
        far_q += [(starts[part] - starts[low], got) for part in range(low, high)]
    for bit in hops:
        other = swap(after(pooled, *pooled_wait), bit)
        pooled = jnp.concatenate([pooled, other], axis=1)
        pooled_wait = others
    done = []
    for part in parts:
        wait = []
        if part == 1:
            bias = after(bias, held[parts[-1]][side][1])
        if part >= 2:
            wait = [done[part - 2][0]]
        if part == 2:
            bias = after(bias, done[0][2])
        for mask in masks[1:]:
            bit = mask & -mask
            if mask != bit:
                start, array = held[part][mask ^ bit]
                if array.shape[1] != sizes[part]:
                    array = array[:, start : start + sizes[part]]
                held[part][mask] = (0, swap(after(array, *wait), bit))
        blocks = [held[part][mask] for mask in masks]
        own_acc, own_stat, code = attend(
            sizes[part], bias, (starts[part], queries), far_q[part], blocks
        )
        done.append((own_acc, own_stat, swap(code, half)))

    coarse_scores = (
        jnp.einsum(
            "hqd,hkd->hqk", pooled_q, pooled[..., :width], preferred_element_type=jnp.float32
        )
        * scale
    )
    coarse_top = jnp.max(coarse_scores, axis=-1, keepdims=True)
    coarse_weights = jnp.exp(coarse_scores - coarse_top).astype(jnp.bfloat16)
    coarse_total = jnp.sum(coarse_weights.astype(jnp.float32), axis=-1)
    coarse_cube = (
        jnp.einsum(
            "hqk,hkd->hqd", coarse_weights, pooled[..., width:], preferred_element_type=jnp.float32
        )
        / coarse_total[..., None]
    )
    kept, received = [], []
    for part in parts:
        own_acc, own_stat, code = done[part]
        if part != parts[-1]:
            code = after(code, done[min(part + 2, parts[-1])][0])
        outs = merge(starts[part], tokens, own_acc, own_stat, code, gate, coarse_cube)
        kept.append(outs[0])
        if split:
            received.append(swap(outs[1], 1))
    kept = jnp.concatenate(kept, axis=0)
    if not split:
        return kept
    received = jnp.concatenate(received, axis=0)
    first = jnp.where(core == 0, kept, received)
    second = jnp.where(core == 0, received, kept)
    return jnp.concatenate([first, second], axis=0)


def solution(mesh):
    in_specs = (
        P("head", "ctx", None),
        P("head", "ctx", None),
        P("head", "ctx", None),
        P("ctx", None),
        P("head", "ctx"),
    )
    out_specs = P("head", "ctx", None)
    return jax.shard_map(
        functools.partial(body, mesh.shape["ctx"]),
        mesh=mesh,
        in_specs=in_specs,
        out_specs=out_specs,
        check_vma=False,
    )
```
